32 devices in a mesh: head: 4 (over x, core), tok: 8 (over z, y).
Axes of the slice: x: 2, y: 2, z: 4, core: 2. Of those that a mesh axis runs over, the one named last changes fastest.
Arguments:
- query_rows: bfloat16 [2, 2048, 1280], P(None, 'tok', 'head'), may hold values from -6 to 6
- key_rows: bfloat16 [2, 2048, 1280], P(None, 'tok', 'head'), may hold values from -6 to 6
- value_rows: bfloat16 [2, 2048, 1280], P(None, 'tok', 'head'), may hold values from -8 to 8
- token_rates: float32 [2, 4, 2048], P(None, 'head', 'tok'), may hold values from 0.1 to 1
- gate_weight: bfloat16 [4, 320, 320], P('head'), may hold values from -0.3125 to 0.3125
- up_weight: bfloat16 [4, 320, 320], P('head'), may hold values from -0.3125 to 0.3125
- down_weight: bfloat16 [4, 320, 320], P('head'), may hold values from -0.3125 to 0.3125
- step_size: float32 [4], P('head'), may hold values from 0.3 to 1
- branch_gains: float32 [2, 1280], replicated, may hold values from 0.1 to 1.9
Outputs:
- block_output: float32 [2, 8, 256, 1280], P(None, 'tok', 'head')
The draws below stay inside these ranges and needn't reach their ends.
All inputs are finite; a program needn't handle non-finite values.
Results may differ from the reference program's by a relative error of at most 0.018.
Values may be sent and summed in bfloat16 or wider, within the bound.
No kernel may reach another device: no remote copies, remote signals or barrier semaphores. Data moves between devices by JAX's collectives and lax.ppermute only.
A program may use at most 64 MiB of HBM per device.

```python
import math
import jax
import jax.numpy as jnp
from jax import lax

DH = 320
NH = 4
D = 1280
SEG_DEV = 256
SEGMENTS = 2
SEG_TOKENS = 2048
WINDOW = 256
NS_STEPS = 3
N_TOK = 8


def draw_query_rows(key, part):
    shape = (SEGMENTS, SEG_TOKENS, D)
    result = jnp.clip(jax.random.normal(jax.random.fold_in(key, 11), shape, jnp.float32), -6.0, 6.0)
    return result.astype(jnp.bfloat16)


def draw_key_rows(key, part):
    shape = (SEGMENTS, SEG_TOKENS, D)
    result = jnp.clip(jax.random.normal(jax.random.fold_in(key, 13), shape, jnp.float32), -6.0, 6.0)
    return result.astype(jnp.bfloat16)


def draw_value_rows(key, part):
    shape = (SEGMENTS, SEG_TOKENS, D)
    column = jnp.arange(D)
    head_scale = 0.6 * 3.0 ** ((column // DH).astype(jnp.float32) / max(NH - 1, 1))
    noise = jax.random.normal(jax.random.fold_in(key, 17), shape, jnp.float32)
    result = jnp.clip(noise, -4.0, 4.0) * head_scale
    return result.astype(jnp.bfloat16)


def level_of(key, dims, cuts, least, high):
    loudness = 1.0
    for axis_at, shards_of in cuts:
        steps = jax.random.uniform(jax.random.fold_in(jax.random.fold_in(key, 6), axis_at), (shards_of,), jnp.float32, least / len(cuts), high / len(cuts))
        loudness = loudness * jnp.repeat(jnp.exp(steps), dims[axis_at] // shards_of).reshape((-1,) + (1,) * (len(dims) - 1 - axis_at))
    return loudness


def centred(stream_key, extent, scale, reach, split=(), held_as=jnp.bfloat16):
    entries = scale * jax.random.normal(stream_key, extent, jnp.float32)
    if split:
        entries = entries * level_of(stream_key, extent, split, -0.22, 0.18)
    return jnp.clip(entries, -reach, reach).astype(held_as)


def setup_inputs(seed: int = 0) -> dict:
    key_of = jax.random.split(jax.random.key(seed), 10)
    return {
        "query_rows": draw_query_rows(jax.random.fold_in(key_of[9], 71), 0),
        "key_rows": draw_key_rows(jax.random.fold_in(key_of[9], 71), 0),
        "value_rows": draw_value_rows(jax.random.fold_in(key_of[9], 71), 0),
        "token_rates": jnp.clip(jnp.exp(math.log(1.0) - 2.3025851 * jax.random.uniform(key_of[3], (SEGMENTS, NH, SEG_TOKENS), jnp.float32) ** level_of(key_of[3], (SEGMENTS, NH, SEG_TOKENS), ((1, 4), (2, 8)), -0.2, 0.2)), 0.1, 1.0),
        "gate_weight": centred(key_of[4], (NH, DH, DH), DH ** -0.5, 0.3125, ((0, 4),)),
        "up_weight": centred(key_of[5], (NH, DH, DH), DH ** -0.5, 0.3125, ((0, 4),)),
        "down_weight": centred(key_of[6], (NH, DH, DH), DH ** -0.5, 0.3125, ((0, 4),)),
        "step_size": jnp.clip(jnp.exp(math.log(1.0) - 1.2039728 * jax.random.uniform(key_of[7], (NH,), jnp.float32) ** level_of(key_of[7], (NH,), ((0, 4),), -0.2, 0.2)), 0.3, 1.0),
        "branch_gains": jnp.clip(1.0 + 0.18 * jax.random.normal(key_of[8], (2, D), jnp.float32), 0.1, 1.9),
    }


NEWTON_A = 3.4445
NEWTON_B = -4.775
NEWTON_C = 2.0315
NORM_EPS = 1e-06
FROB_EPS = 1e-07

def product(left, right):
    return jnp.dot(left, right, preferred_element_type=jnp.float32)

def batched(form, left, right):
    return jnp.einsum(form, left.astype(jnp.float32), right.astype(jnp.float32), precision=lax.Precision.HIGHEST)

def gradients(key_head, value_head, rate_head, weights):
    pre_gate = product(key_head, weights[0])
    pre_up = product(key_head, weights[1])
    sig_gate = jax.nn.sigmoid(pre_gate)
    swish = pre_gate * sig_gate
    hidden = (swish * pre_up).astype(jnp.bfloat16)
    target = (-(rate_head[:, None] * value_head.astype(jnp.float32))).astype(jnp.bfloat16)
    grad_down = product(hidden.T, target)
    backward = product(target, weights[2].T)
    d_gate = (backward * pre_up * sig_gate * (1.0 + pre_gate * (1.0 - sig_gate))).astype(jnp.bfloat16)
    d_up = (backward * swish).astype(jnp.bfloat16)
    return jnp.stack([product(key_head.T, d_gate), product(key_head.T, d_up), grad_down])

def orthogonalize(stacked):
    norms = jnp.sqrt(lax.optimization_barrier(jnp.sum(stacked * stacked, axis=(1, 2), keepdims=True)))
    iterate = (stacked / (norms + FROB_EPS)).astype(jnp.bfloat16)
    for sweep_index in range(NS_STEPS):
        square = batched('mij,mkj->mik', iterate, iterate).astype(jnp.bfloat16)
        mixing = (NEWTON_B * square.astype(jnp.float32) + NEWTON_C * batched('mij,mjk->mik', square, square)).astype(jnp.bfloat16)
        iterate = (NEWTON_A * iterate.astype(jnp.float32) + batched('mij,mjk->mik', mixing, iterate)).astype(jnp.bfloat16)
    return iterate

def apply_fast(query_head, weights):
    gate = product(query_head, weights[0])
    up_part = product(query_head, weights[1])
    hidden = (jax.nn.silu(gate) * up_part).astype(jnp.bfloat16)
    return product(hidden, weights[2]).astype(jnp.bfloat16)

def one_head(packed):
    query_head, key_head, value_head, rate_head, gate_head, up_head, down_head, step_head = packed
    weights = jnp.stack([gate_head, up_head, down_head])
    outputs = []
    for section_index in range(SEGMENTS):
        update = orthogonalize(gradients(key_head[section_index], value_head[section_index], rate_head[section_index], weights))
        weights = (weights.astype(jnp.float32) - step_head * update.astype(jnp.float32)).astype(jnp.bfloat16)
        outputs.append(apply_fast(query_head[section_index], weights))
    return jnp.stack(outputs)

def split_heads(array):
    return array.reshape(SEGMENTS, SEG_TOKENS, NH, DH).transpose(2, 0, 1, 3)

def window_attention(query_rows, key_rows, value_rows):
    total_rows = SEGMENTS * SEG_TOKENS
    flat_query = query_rows.reshape(total_rows, NH, DH)
    padding = jnp.zeros((WINDOW, NH, DH), jnp.bfloat16)
    flat_key = jnp.concatenate([padding, key_rows.reshape(total_rows, NH, DH)], 0)
    flat_value = jnp.concatenate([padding, value_rows.reshape(total_rows, NH, DH)], 0)
    block_rows = math.gcd(total_rows, 512)
    scale = 1.0 / math.sqrt(DH)

    def one_block(block_number):
        start = (block_number * block_rows).astype(jnp.int32)
        query_block = lax.dynamic_slice_in_dim(flat_query, start, block_rows, 0)
        key_block = lax.dynamic_slice_in_dim(flat_key, start, block_rows + WINDOW, 0)
        value_block = lax.dynamic_slice_in_dim(flat_value, start, block_rows + WINDOW, 0)
        scores = batched('qhd,khd->hqk', query_block, key_block) * scale
        query_index = jnp.arange(block_rows, dtype=jnp.int32)[:, None]
        key_index = jnp.arange(block_rows + WINDOW, dtype=jnp.int32)[None, :]
        live = (key_index > query_index) & (key_index <= query_index + WINDOW) & (start + key_index >= WINDOW)
        scores = jnp.where(live[None], scores, -1e+30)
        top = lax.optimization_barrier(jnp.max(scores, axis=-1, keepdims=True))
        expo = jnp.exp(scores - top)
        probs = (expo / lax.optimization_barrier(jnp.sum(expo, axis=-1, keepdims=True))).astype(jnp.bfloat16)
        return batched('hqk,khd->qhd', probs, value_block).astype(jnp.bfloat16)
    blocks = lax.map(one_block, jnp.arange(total_rows // block_rows, dtype=jnp.int32))
    return blocks.reshape(SEGMENTS, SEG_TOKENS, NH * DH)

def normalize(branch, gain):
    widened = branch.astype(jnp.float32)
    mean_square = lax.optimization_barrier(jnp.sum(widened * widened, axis=-1, keepdims=True)) / D
    return widened * lax.rsqrt(mean_square + NORM_EPS) * gain

def reference(query_rows, key_rows, value_rows, token_rates, gate_weight, up_weight, down_weight, step_size, branch_gains):
    packed = (split_heads(query_rows), split_heads(key_rows), split_heads(value_rows), token_rates.transpose(1, 0, 2), gate_weight, up_weight, down_weight, step_size)
    fast_heads = lax.map(one_head, packed)
    fast = fast_heads.transpose(1, 2, 0, 3).reshape(SEGMENTS, SEG_TOKENS, D)
    attended = window_attention(query_rows, key_rows, value_rows)
    combined = normalize(fast, branch_gains[0]) + normalize(attended, branch_gains[1])
    return combined.reshape(SEGMENTS, N_TOK, SEG_DEV, D)
```

```python
import math

import jax
import jax.numpy as jnp
from jax import lax
from jax.sharding import PartitionSpec as P

WINDOW = 256
NS_STEPS = 3
NEWTON_A = 3.4445
NEWTON_B = -4.775
NEWTON_C = 2.0315
NORM_EPS = 1e-06
FROB_EPS = 1e-07
BOTH = ("head", "tok")
RATE_ROWS = 16


def moved(array, heads, toks, where):
    pairs = []
    for h in range(heads):
        for t in range(toks):
            to_h, to_t = where(h, t)
            pairs.append((h * toks + t, to_h * toks + to_t))
    return lax.ppermute(array, BOTH, pairs)


def product(left, right):
    return jnp.dot(left, right, preferred_element_type=jnp.float32)


def over_tokens(left, right):
    return lax.dot_general(
        left, right, (((0,), (0,)), ((), ())), preferred_element_type=jnp.float32
    )


def gradients(keys, values, rates, weights):
    pre_gate = product(keys, weights[0])
    pre_up = product(keys, weights[1])
    sig_gate = jax.nn.sigmoid(pre_gate)
    swish = pre_gate * sig_gate
    hidden = (swish * pre_up).astype(jnp.bfloat16)
    target = (-(rates[:, None] * values.astype(jnp.float32))).astype(jnp.bfloat16)
    grad_down = over_tokens(hidden, target)
    backward = lax.dot_general(
        target, weights[2], (((1,), (1,)), ((), ())), preferred_element_type=jnp.float32
    )
    d_gate = (backward * pre_up * sig_gate * (1.0 + pre_gate * (1.0 - sig_gate))).astype(
        jnp.bfloat16
    )
    d_up = (backward * swish).astype(jnp.bfloat16)
    return jnp.stack([over_tokens(keys, d_gate), over_tokens(keys, d_up), grad_down])


def local_orthogonalize(stacked):
    norms = jnp.sqrt(jnp.sum(stacked * stacked, axis=(1, 2), keepdims=True))
    iterate = (stacked / (norms + FROB_EPS)).astype(jnp.bfloat16)
    for _ in range(NS_STEPS):
        square = jnp.einsum(
            "mij,mkj->mik", iterate, iterate, preferred_element_type=jnp.float32
        ).astype(jnp.bfloat16)
        mixing = (
            NEWTON_B * square.astype(jnp.float32)
            + NEWTON_C
            * jnp.einsum("mij,mjk->mik", square, square, preferred_element_type=jnp.float32)
        ).astype(jnp.bfloat16)
        iterate = (
            NEWTON_A * iterate.astype(jnp.float32)
            + jnp.einsum("mij,mjk->mik", mixing, iterate, preferred_element_type=jnp.float32)
        ).astype(jnp.bfloat16)
    return iterate


def apply_fast(query_part, weights):
    gate = product(query_part, weights[0])
    up_part = product(query_part, weights[1])
    hidden = (jax.nn.silu(gate) * up_part).astype(jnp.bfloat16)
    return product(hidden, weights[2]).astype(jnp.bfloat16)


def attention(query, prev, own, prev_live):
    rows, width = query.shape
    keys = jnp.concatenate([prev[:rows, :width], own[:rows, :width]], 0)
    values = jnp.concatenate([prev[:rows, width:], own[:rows, width:]], 0)
    scores = lax.dot_general(
        query, keys, (((1,), (1,)), ((), ())), preferred_element_type=jnp.float32
    ) * (1.0 / math.sqrt(width))
    query_index = jnp.arange(rows)[:, None]
    key_index = jnp.arange(2 * rows)[None, :]
    band = (key_index > query_index) & (key_index <= query_index + WINDOW)
    live = band & ((key_index >= WINDOW) | prev_live)
    scores = jnp.where(live, scores, -1e30)
    top = jnp.max(scores, axis=-1, keepdims=True)
    expo = jnp.exp(scores - top)
    probs = (expo / jnp.sum(expo, axis=-1, keepdims=True)).astype(jnp.bfloat16)
    return product(probs, values).astype(jnp.bfloat16)


def packed_block(keys, values, rates):
    width = keys.shape[1]
    high = lax.reduce_precision(rates, 8, 7)
    middle = lax.reduce_precision(rates - high, 8, 7)
    low = lax.reduce_precision(rates - high - middle, 8, 7)
    terms = jnp.stack([high, middle, low]).astype(jnp.bfloat16)
    terms = jnp.pad(terms, ((0, RATE_ROWS - 3), (0, 2 * width - rates.shape[0])))
    return jnp.concatenate([jnp.concatenate([keys, values], 1), terms], 0)


def block_rates(block, rows):
    terms = block[rows : rows + 3, :rows].astype(jnp.float32)
    return terms[0] + terms[1] + terms[2]


def on_device(
    query_rows,
    key_rows,
    value_rows,
    token_rates,
    gate_weight,
    up_weight,
    down_weight,
    step_size,
    branch_gains,
    *,
    heads,
    toks,
):
    segments, rows, width = query_rows.shape
    half = toks // 2
    full_width = width * heads

    def regroup(h, t):
        return h - h % 2 + t // half, (h % 2) * half + t % half

    def other_core(h, t):
        return h ^ 1, t

    def send(array, where):
        return moved(array, heads, toks, where)

    blocks = [
        packed_block(key_rows[s], value_rows[s], token_rates[s, 0]) for s in range(segments)
    ]
    own = [send(block, regroup) for block in blocks]
    queries = send(query_rows, regroup)
    weights = jnp.stack([gate_weight[0], up_weight[0], down_weight[0]])
    core = lax.axis_index("head") % 2
    tok = lax.axis_index("tok")
    group = tok // half
    place = tok % half
    other_weights = send(weights, other_core)
    weights = jnp.where(core == group, weights, other_weights)
    steps = step_size[0]
    steps = jnp.where(core == group, steps, send(step_size, other_core)[0])

    outputs, attended = [], []
    held = []
    for s in range(segments):
        here = [own[s]]
        for mask in range(1, half):
            here.append(send(own[s], lambda h, t, mask=mask: (h, t ^ mask)))
        there = [send(block, other_core) for block in here]
        held.append((here, there))

    for s in range(segments):
        here, there = held[s]
        everything = here + there
        keys = jnp.concatenate([b[:rows, :width] for b in everything], 0)
        values = jnp.concatenate([b[:rows, width:] for b in everything], 0)
        rates = jnp.concatenate([block_rates(b, rows) for b in everything], 0)
        update = local_orthogonalize(gradients(keys, values, rates, weights))
        weights = (weights.astype(jnp.float32) - steps * update.astype(jnp.float32)).astype(
            jnp.bfloat16
        )
        outputs.append(apply_fast(queries[s], weights))
        prev = there[half - 1]
        if s > 0:
            prev = jnp.where(core == 0, held[s - 1][1][half - 1], prev)
        mask = 1
        while mask < half:
            prev = jnp.where((place ^ (place - 1)) == mask, here[mask], prev)
            mask = 2 * mask + 1
        prev_live = (s > 0) | (core > 0) | (place > 0)
        attended.append(attention(queries[s], prev, own[s], prev_live))

    share = rows // heads
    head_of = (lax.axis_index("head") - core) + group

    def spread(array):
        parts = array.reshape(heads, share, array.shape[-1])
        got = []
        for shift in range(heads):
            to = (head_of + shift) % heads

            def where(h, t, shift=shift):
                mine = h - h % 2 + t // half
                return (mine + shift) % heads, (h % 2) * half + t % half

            got.append(send(lax.dynamic_index_in_dim(parts, to, 0, False), where))
        stacked = jnp.stack(got)
        me = lax.axis_index("head")
        return jnp.concatenate(
            [
                lax.dynamic_index_in_dim(stacked, (me - j) % heads, 0, False)
                for j in range(heads)
            ],
            -1,
        )

    def normed(branch, gain):
        wide = branch.astype(jnp.float32)
        total = jnp.sum(wide * wide, axis=-1, keepdims=True)
        return wide * lax.rsqrt(total / full_width + NORM_EPS) * gain

    mixed = []
    for s in range(segments):
        mixed.append(
            normed(spread(outputs[s]), branch_gains[0])
            + normed(spread(attended[s]), branch_gains[1])
        )
    return jnp.stack(mixed)[:, None]


def solution(mesh):
    placed = (
        P(None, "tok", "head"),
        P(None, "tok", "head"),
        P(None, "tok", "head"),
        P(None, "head", "tok"),
        P("head", None, None),
        P("head", None, None),
        P("head", None, None),
        P("head"),
        P(),
    )
    heads, toks = mesh.shape["head"], mesh.shape["tok"]

    def program(*arrays):
        return on_device(*arrays, heads=heads, toks=toks)

    return jax.shard_map(
        program,
        mesh=mesh,
        in_specs=placed,
        out_specs=P(None, "tok", "head", None),
        check_vma=False,
    )
```

```python
import functools
import math

import jax
import jax.numpy as jnp
from jax import lax
from jax.experimental import pallas as pl
from jax.experimental.pallas import tpu as pltpu
from jax.sharding import PartitionSpec as P

WINDOW = 256
NS_STEPS = 3
NEWTON_A = 3.4445
NEWTON_B = -4.775
NEWTON_C = 2.0315
NORM_EPS = 1e-06
FROB_EPS = 1e-07
BOTH = ("head", "tok")
EXTRA = 16
VMEM_BYTES = 20 * 1024 * 1024
F32 = jnp.float32
BF16 = jnp.bfloat16


def moved(array, heads, toks, where):
    pairs = []
    for h in range(heads):
        for t in range(toks):
            to = where(h, t)
            if to is not None:
                pairs.append((h * toks + t, to[0] * toks + to[1]))
    return lax.ppermute(array, BOTH, pairs)


def after(arrays, others):
    return lax.optimization_barrier((arrays, others))[0]


def turned(array):
    return jnp.swapaxes(array, 1, 2)


def dot_nn(left, right):
    return jnp.dot(left, right, preferred_element_type=F32)


def dot_nt(left, right):
    return lax.dot_general(left, right, (((1,), (1,)), ((), ())), preferred_element_type=F32)


def call(kernel, out_shape, args, scratch=(), smem=(), loose=(), vmem=VMEM_BYTES, flops=0):
    def space(i):
        return pltpu.SMEM if i in smem else pl.ANY if i in loose else pltpu.VMEM

    specs = [pl.BlockSpec(memory_space=space(i)) for i in range(len(args))]
    return pl.pallas_call(
        kernel,
        out_shape=out_shape,
        in_specs=specs,
        out_specs=jax.tree.map(lambda _: pl.BlockSpec(memory_space=pltpu.VMEM), out_shape),
        scratch_shapes=list(scratch),
        compiler_params=pltpu.CompilerParams(vmem_limit_bytes=vmem),
        cost_estimate=pl.CostEstimate(flops=flops, bytes_accessed=1 << 20, transcendentals=0),
    )(*args)


def pack_kernel(segments, key_ref, value_ref, rate_ref, step_ref, *refs):
    outs, sems = refs[:segments], refs[segments]
    width, rows = key_ref.shape[1:]
    copies = []
    for s, out_ref in enumerate(outs):
        for i, ref in enumerate((key_ref, value_ref)):
            copies.append(
                pltpu.make_async_copy(
                    ref.at[s], out_ref.at[pl.ds(i * width, width)], sems.at[s, i]
                )
            )
    for copy in copies:
        copy.start()
    for s, out_ref in enumerate(outs):
        rate = rate_ref[s]
        step = jnp.full_like(rate, step_ref[0])
        row = lax.broadcasted_iota(jnp.int32, (EXTRA, rows), 0)
        filled = jnp.zeros((EXTRA, rows), F32)
        at = 0
        for value in (rate, step):
            for _ in range(3):
                term = value.astype(BF16).astype(F32)
                filled = jnp.where(row == at, term, filled)
                value = value - term
                at += 1
        out_ref[2 * width :] = filled.astype(BF16)
    for copy in copies:
        copy.wait()


def weight_kernel(gate_ref, up_ref, down_ref, out_ref):
    width = down_ref.shape[0]
    for i, ref in enumerate((gate_ref, up_ref)):
        out_ref[i * width : (i + 1) * width, :width] = ref[...].T
    out_ref[2 * width :, :width] = down_ref[...]
    out_ref[:, width:] = jnp.zeros((3 * width, out_ref.shape[1] - width), BF16)


def add_gradients(blocks, weights, total_ref):
    width = weights.shape[1]
    first = True
    for block in blocks:
        keys = block[:width]
        values = block[width : 2 * width]
        terms = block[2 * width :].astype(F32)
        rate = -(terms[0:1] + terms[1:2] + terms[2:3])
        both = dot_nn(weights[: 2 * width], keys)
        gate, up = both[:width], both[width:]
        back = dot_nn(weights[2 * width :], values) * rate
        sig = jax.nn.sigmoid(gate)
        swish = gate * sig
        hidden = (swish * up * rate).astype(BF16)
        d_gate = (back * up * (sig + swish * (1.0 - sig))).astype(BF16)
        d_up = (back * swish).astype(BF16)
        parts = (dot_nt(d_gate, keys), dot_nt(d_up, keys), dot_nt(hidden, values))
        for i, part in enumerate(parts):
            at = pl.ds(i * width, width)
            total_ref[at] = part if first else total_ref[at] + part
        first = False


def orthogonalized(stacked, width):
    iterates = []
    for i in range(3):
        one = stacked[i * width : (i + 1) * width]
        norm = jnp.sqrt(jnp.sum(one * one, keepdims=True))
        iterates.append((one / (norm + FROB_EPS)).astype(BF16))
    for _ in range(NS_STEPS):
        squares = [dot_nt(x, x).astype(BF16) for x in iterates]
        mixings = [
            (NEWTON_B * s.astype(F32) + NEWTON_C * dot_nn(s, s)).astype(BF16) for s in squares
        ]
        iterates = [
            (NEWTON_A * x.astype(F32) + dot_nn(m, x)).astype(BF16)
            for m, x in zip(mixings, iterates)
        ]
    return iterates


def updated(mine, other, weights, step_block, out_ref):
    width = out_ref.shape[1]
    terms = step_block[2 * width :].astype(F32)
    step = (terms[3:4] + terms[4:5] + terms[5:6])[:, 0:1]
    total = mine[:, :width].astype(F32) + other[:, :width].astype(F32)
    for i, x in enumerate(orthogonalized(total, width)):
        at = pl.ds(i * width, width)
        out_ref[at] = (weights[at].astype(F32) - step * x.astype(F32)).astype(BF16)


def write_sum(total_ref, out_ref):
    width = total_ref.shape[1]
    out_ref[:, :width] = total_ref[...].astype(BF16)
    out_ref[:, width:] = jnp.zeros((out_ref.shape[0], out_ref.shape[1] - width), BF16)


def fast_rows(query, weights):
    width = weights.shape[1]
    both = dot_nt(query, weights[: 2 * width])
    gate, up = both[:, :width], both[:, width:]
    hidden = (gate * jax.nn.sigmoid(gate) * up).astype(BF16)
    return dot_nn(hidden, weights[2 * width :]).astype(BF16)


def first_kernel(count, place_ref, *refs):
    blocks = refs[:count]
    mine, other, held_ref, out_ref, total_ref = refs[count:]
    width = held_ref.shape[1]
    held_ref[...] = jnp.where(place_ref[3] == 1, mine[:, :width], other[:, :width])
    add_gradients(blocks, held_ref, total_ref)
    write_sum(total_ref, out_ref)


def update_kernel(mine, other, weight_ref, block, next_ref):
    updated(mine, other, weight_ref, block, next_ref)


def middle_kernel(count, *refs):
    blocks, (weight_ref, out_ref, total_ref) = refs[:count], refs[count:]
    add_gradients(blocks, weight_ref, total_ref)
    write_sum(total_ref, out_ref)


def last_kernel(heads, place_ref, mine, other, weight_ref, block, query_ref, *refs):
    outs, (next_ref, fast_ref) = refs[:heads], refs[heads:]
    updated(mine, other, weight_ref, block, next_ref)
    fast_ref[...] = fast_rows(query_ref[...], next_ref)
    share = fast_ref.shape[0] // heads
    for shift in range(heads):
        to = lax.rem(place_ref[0] + shift, heads)
        outs[shift][...] = fast_ref[pl.ds(pl.multiple_of(to * share, share), share)]


def query_kernel(heads, segments, choices, *refs):
    place_ref, query_ref = refs[:2]
    weight_refs = refs[2 : 1 + segments]
    at = 1 + segments
    owns = refs[at : at + segments]
    at += segments
    cands = [refs[at + s * choices : at + (s + 1) * choices] for s in range(segments)]
    at += segments * choices
    outs = refs[at : at + heads]
    last_query_ref, rows_ref = refs[at + heads :]
    head, place, core = place_ref[0], place_ref[1], place_ref[2]
    width, rows = query_ref.shape[1:]
    share = rows // heads
    scale = 1.0 / math.sqrt(width)
    for s in range(segments):
        query = query_ref[s].T
        if s == segments - 1:
            last_query_ref[...] = query
        else:
            rows_ref[segments + s] = fast_rows(query, weight_refs[s])
        prev = cands[s][choices - 1][: 2 * width]
        if s > 0:
            prev = jnp.where(core == 0, cands[s - 1][choices - 1][: 2 * width], prev)
        for i in range(choices - 1):
            low = lax.rem(place, 2 << i) == (1 << i)
            prev = jnp.where(low, cands[s][i][: 2 * width], prev)
        own = owns[s]
        own_scores = dot_nn(query, own[:width]) * scale
        prev_scores = dot_nn(query, prev[:width]) * scale
        q_at = lax.broadcasted_iota(jnp.int32, (rows, rows), 0)
        k_at = lax.broadcasted_iota(jnp.int32, (rows, rows), 1)
        own_live = (k_at <= q_at) & (k_at > q_at - WINDOW)
        prev_live = k_at - rows > q_at - WINDOW
        if s == 0:
            reach = jnp.where((core == 0) & (place == 0), -rows, 0)
            prev_live = prev_live & (k_at < rows + reach)
        own_scores = jnp.where(own_live, own_scores, -1e30)
        prev_scores = jnp.where(prev_live, prev_scores, -1e30)
        top = jnp.maximum(
            jnp.max(own_scores, axis=-1, keepdims=True),
            jnp.max(prev_scores, axis=-1, keepdims=True),
        )
        own_expo = jnp.exp(own_scores - top)
        prev_expo = jnp.exp(prev_scores - top)
        total = jnp.sum(own_expo, axis=-1, keepdims=True) + jnp.sum(
            prev_expo, axis=-1, keepdims=True
        )
        over = 1.0 / total
        attended = dot_nt((own_expo * over).astype(BF16), own[width : 2 * width]) + dot_nt(
            (prev_expo * over).astype(BF16), prev[width:]
        )
        rows_ref[s] = attended.astype(BF16)
    for shift in range(heads):
        to = lax.rem(head + shift, heads)
        for i in range(2 * segments - 1):
            outs[shift][i] = rows_ref[i, pl.ds(pl.multiple_of(to * share, share), share)]


def normed(parts, gain_row, full_width):
    total = 0.0
    wides = []
    for part in parts:
        wide = part.astype(F32)
        wides.append(wide)
        total = total + jnp.sum(wide * wide, axis=-1, keepdims=True)
    factor = lax.rsqrt(total / full_width + NORM_EPS)
    width = parts[0].shape[1]
    return [
        wide * factor * gain_row[:, i * width : (i + 1) * width] for i, wide in enumerate(wides)
    ]


def final_kernel(heads, segments, me_ref, gain_ref, *refs):
    early, late, out_ref = refs[:heads], refs[heads : 2 * heads], refs[2 * heads]
    held = refs[2 * heads + 1]
    share, width = late[0].shape
    me = me_ref[0]
    for k in range(heads):
        at = lax.rem(me - k + heads, heads)
        held[at, : 2 * segments - 1] = early[k][...]
        held[at, 2 * segments - 1] = late[k][...]
    for s in range(segments):
        fast = normed([held[j, segments + s] for j in range(heads)], gain_ref[0:1], heads * width)
        att = normed([held[j, s] for j in range(heads)], gain_ref[1:2], heads * width)
        out_ref[s, 0] = jnp.concatenate([a + b for a, b in zip(fast, att)], -1)


def on_device(
    query_rows,
    key_rows,
    value_rows,
    token_rates,
    gate_weight,
    up_weight,
    down_weight,
    step_size,
    branch_gains,
    *,
    heads,
    toks,
):
    segments, rows, width = query_rows.shape
    half = toks // 2
    share = rows // heads

    def regroup(h, t):
        return h - h % 2 + t // half, (h % 2) * half + t % half

    def other_core(h, t):
        return h ^ 1, t

    def send(array, where):
        return moved(array, heads, toks, where)

    me = lax.axis_index("head")
    core = me % 2
    tok = lax.axis_index("tok")
    group = tok // half
    place = tok % half
    head_of = me - core + group

    position = jnp.stack([head_of, place, core, (core == group).astype(jnp.int32)])
    position = position.astype(jnp.int32)
    block_shape = jax.ShapeDtypeStruct((2 * width + EXTRA, rows), BF16)
    blocks = call(
        functools.partial(pack_kernel, segments),
        (block_shape,) * segments,
        (turned(key_rows), turned(value_rows), token_rates, step_size),
        (pltpu.SemaphoreType.DMA((segments, 2)),),
        smem=(3,),
        loose=(0, 1),
        vmem=56 * 1024 * 1024,
    )
    own = [send(block, regroup) for block in blocks]
    padded = -(-width // 128) * 128
    stacked = call(
        weight_kernel,
        jax.ShapeDtypeStruct((3 * width, padded), BF16),
        after((gate_weight[0], up_weight[0], down_weight[0]), blocks),
    )
    lent = send(
        stacked, lambda h, t: (h ^ 1, t) if h % 2 == t // half else None
    )
    queries = send(turned(query_rows), regroup)

    here = []
    for s in range(segments):
        here.append(
            [own[s]]
            + [
                send(own[s], lambda h, t, mask=mask: (h, t ^ mask)) for mask in range(1, half)
            ]
        )

    grad_shape = jax.ShapeDtypeStruct((3 * width, padded), BF16)
    weight_shape = jax.ShapeDtypeStruct((3 * width, width), BF16)
    total = pltpu.VMEM((3 * width, width), F32)
    grad_flops = 2 * 6 * half * rows * width * width
    ns_flops = 2 * 27 * width**3

    weights, mine = call(
        functools.partial(first_kernel, half),
        (weight_shape, grad_shape),
        (position, *after(here[0], own), stacked, lent),
        (total,),
        smem=(0,),
        flops=grad_flops,
    )
    all_weights = []
    for s in range(1, segments):
        other = send(mine, other_core)
        if s == 1:
            other, queries = lax.optimization_barrier((other, queries))
        weights = call(
            update_kernel, weight_shape, (mine, other, weights, own[s - 1]), flops=ns_flops
        )
        mine = call(
            functools.partial(middle_kernel, half),
            grad_shape,
            (*here[s], weights),
            (total,),
            flops=grad_flops,
        )
        all_weights.append(weights)
    other = send(mine, other_core)

    lasts = [
        send(here[s][half - 1], lambda h, t: (h ^ 1, t) if t % half == 0 else None)
        for s in range(segments)
    ]
    cands = []
    for s in range(segments):
        one = []
        mask = 1
        while mask < half:
            one.append(here[s][mask])
            mask = 2 * mask + 1
        cands.append(one + [lasts[s]])
    choices = len(cands[0])
    *early, last_query = call(
        functools.partial(query_kernel, heads, segments, choices),
        tuple(
            jax.ShapeDtypeStruct((2 * segments - 1, share, width), BF16) for _ in range(heads)
        )
        + (jax.ShapeDtypeStruct((rows, width), BF16),),
        (position, queries, *all_weights, *own, *[c for one in cands for c in one]),
        (pltpu.VMEM((2 * segments - 1, rows, width), BF16),),
        smem=(0,),
        flops=2 * segments * 4 * rows * rows * width,
    )
    late = call(
        functools.partial(last_kernel, heads),
        tuple(jax.ShapeDtypeStruct((share, width), BF16) for _ in range(heads)),
        (position, mine, other, weights, own[-1], last_query),
        (pltpu.VMEM((3 * width, width), BF16), pltpu.VMEM((rows, width), BF16)),
        smem=(0,),
        flops=ns_flops,
    )

    def spread(parts):
        got = []
        for shift in range(heads):

            def where(h, t, shift=shift):
                mine = h - h % 2 + t // half
                return (mine + shift) % heads, (h % 2) * half + t % half

            got.append(send(parts[shift], where))
        return got

    return call(
        functools.partial(final_kernel, heads, segments),
        jax.ShapeDtypeStruct((segments, 1, share, heads * width), F32),
        (me[None].astype(jnp.int32), branch_gains, *spread(early), *spread(late)),
        (pltpu.VMEM((heads, 2 * segments, share, width), BF16),),
        smem=(0,),
    )


def solution(mesh):
    placed = (
        P(None, "tok", "head"),
        P(None, "tok", "head"),
        P(None, "tok", "head"),
        P(None, "head", "tok"),
        P("head", None, None),
        P("head", None, None),
        P("head", None, None),
        P("head"),
        P(),
    )
    heads, toks = mesh.shape["head"], mesh.shape["tok"]

    def program(*arrays):
        return on_device(*arrays, heads=heads, toks=toks)

    return jax.shard_map(
        program,
        mesh=mesh,
        in_specs=placed,
        out_specs=P(None, "tok", "head", None),
        check_vma=False,
    )
```

```python
import functools
import math

import jax
import jax.numpy as jnp
from jax import lax
from jax.experimental import pallas as pl
from jax.experimental.pallas import tpu as pltpu
from jax.sharding import PartitionSpec as P

WINDOW = 256
NS_STEPS = 3
NEWTON_A = 3.4445
NEWTON_B = -4.775
NEWTON_C = 2.0315
NORM_EPS = 1e-06
FROB_EPS = 1e-07
BOTH = ("head", "tok")
EXTRA = 16
VMEM_BYTES = 20 * 1024 * 1024
F32 = jnp.float32
BF16 = jnp.bfloat16


def moved(array, heads, toks, where):
    pairs = []
    for h in range(heads):
        for t in range(toks):
            to = where(h, t)
            if to is not None:
                pairs.append((h * toks + t, to[0] * toks + to[1]))
    return lax.ppermute(array, BOTH, pairs)


def hold_kernel(in_ref, out_ref):
    out_ref[...] = in_ref[...]


def tied(array, *others):
    shape = jax.ShapeDtypeStruct(array.shape, array.dtype)
    return call(hold_kernel, shape, (array,), waits=others)


def turned(array):
    return jnp.swapaxes(array, 1, 2)


def dot_nn(left, right):
    return jnp.dot(left, right, preferred_element_type=F32)


def dot_nt(left, right):
    return lax.dot_general(left, right, (((1,), (1,)), ((), ())), preferred_element_type=F32)


def call(
    kernel,
    out_shape,
    args,
    scratch=(),
    smem=(),
    loose=(),
    loose_out=(),
    aliases={},
    waits=(),
    vmem=VMEM_BYTES,
    flops=0,
):
    def space(i):
        return pltpu.SMEM if i in smem else pl.ANY if i in loose else pltpu.VMEM

    count = len(args)
    specs = [pl.BlockSpec(memory_space=space(i)) for i in range(count)]
    specs += [pl.BlockSpec(memory_space=pltpu.VMEM) for _ in waits]
    single = not isinstance(out_shape, tuple)
    shapes = (out_shape,) if single else out_shape

    def body(*refs):
        kernel(*refs[:count], *refs[count + len(waits) :])

    outs = pl.pallas_call(
        body,
        out_shape=shapes,
        in_specs=specs,
        out_specs=tuple(
            pl.BlockSpec(memory_space=pl.ANY if i in loose_out else pltpu.VMEM)
            for i in range(len(shapes))
        ),
        scratch_shapes=list(scratch),
        input_output_aliases=aliases,
        compiler_params=pltpu.CompilerParams(vmem_limit_bytes=vmem),
        cost_estimate=pl.CostEstimate(flops=flops, bytes_accessed=1 << 20, transcendentals=0),
    )(*args, *waits)
    return outs[0] if single else outs


def pack_kernel(segments, key_ref, value_ref, rate_ref, step_ref, *refs):
    outs, (held_rate, held_step, sems) = refs[:segments], refs[segments:]
    width, rows = key_ref.shape[1:]
    copies = [
        pltpu.make_async_copy(rate_ref, held_rate, sems.at[segments, 0]),
        pltpu.make_async_copy(step_ref, held_step, sems.at[segments, 1]),
    ]
    for s, out_ref in enumerate(outs):
        for i, ref in enumerate((key_ref, value_ref)):
            copies.append(
                pltpu.make_async_copy(
                    ref.at[s], out_ref.at[pl.ds(i * width, width)], sems.at[s, i]
                )
            )
    for copy in copies:
        copy.start()
    for copy in copies[:2]:
        copy.wait()
    for s, out_ref in enumerate(outs):
        rate = held_rate[s]
        step = jnp.full_like(rate, held_step[0])
        row = lax.broadcasted_iota(jnp.int32, (EXTRA, rows), 0)
        filled = jnp.zeros((EXTRA, rows), F32)
        at = 0
        for value in (rate, step):
            for _ in range(3):
                term = value.astype(BF16).astype(F32)
                filled = jnp.where(row == at, term, filled)
                value = value - term
                at += 1
        out_ref[2 * width :] = filled.astype(BF16)
    for copy in copies[2:]:
        copy.wait()


def weight_kernel(place_ref, *refs):
    mine, other, (out_ref, held, sems) = refs[:3], refs[3:6], refs[6:]
    width = out_ref.shape[1]

    def load(parts):
        copies = [
            pltpu.make_async_copy(ref, held.at[i], sems.at[i]) for i, ref in enumerate(parts)
        ]
        for copy in copies:
            copy.start()
        for copy in copies:
            copy.wait()

    @pl.when(place_ref[3] == 1)
    def _():
        load(mine)

    @pl.when(place_ref[3] != 1)
    def _():
        load(other)

    for i in range(3):
        out_ref[i * width : (i + 1) * width] = held[i].T if i < 2 else held[i]


def add_gradients(blocks, weights, total_ref, first=True):
    width = weights.shape[1]
    for block in blocks:
        keys = block[:width]
        values = block[width : 2 * width]
        terms = block[2 * width :].astype(F32)
        rate = -(terms[0:1] + terms[1:2] + terms[2:3])
        both = dot_nn(weights[: 2 * width], keys)
        gate, up = both[:width], both[width:]
        back = dot_nn(weights[2 * width :], values) * rate
        sig = jax.nn.sigmoid(gate)
        swish = gate * sig
        hidden = (swish * up * rate).astype(BF16)
        d_gate = (back * up * (sig + swish * (1.0 - sig))).astype(BF16)
        d_up = (back * swish).astype(BF16)
        parts = (dot_nt(d_gate, keys), dot_nt(d_up, keys), dot_nt(hidden, values))
        for i, part in enumerate(parts):
            at = pl.ds(i * width, width)
            total_ref[at] = part if first else total_ref[at] + part
        first = False


def orthogonalized(totals):
    iterates = []
    for one in totals:
        norm = jnp.sqrt(jnp.sum(one * one, keepdims=True))
        iterates.append((one / (norm + FROB_EPS)).astype(BF16))
    for _ in range(NS_STEPS):
        squares = [dot_nt(x, x).astype(BF16) for x in iterates]
        mixings = [
            (NEWTON_B * s.astype(F32) + NEWTON_C * dot_nn(s, s)).astype(BF16) for s in squares
        ]
        iterates = [
            (NEWTON_A * x.astype(F32) + dot_nn(m, x)).astype(BF16)
            for m, x in zip(mixings, iterates)
        ]
    return iterates


def updated(mine, other, weights, step_block, out_ref):
    width = out_ref.shape[1]
    terms = step_block[2 * width :].astype(F32)
    step = (terms[3:4] + terms[4:5] + terms[5:6])[:, 0:1]
    totals = [a[:, :width].astype(F32) + b[:, :width].astype(F32) for a, b in zip(mine, other)]
    for i, x in enumerate(orthogonalized(totals)):
        at = pl.ds(i * width, width)
        out_ref[at] = (weights[at].astype(F32) - step * x.astype(F32)).astype(BF16)


def write_sums(total_ref, outs):
    width = total_ref.shape[1]
    for i, out_ref in enumerate(outs):
        out_ref[:, :width] = total_ref[i * width : (i + 1) * width].astype(BF16)
        out_ref[:, width:] = jnp.zeros((width, out_ref.shape[1] - width), BF16)


def fast_rows(query, weights):
    width = weights.shape[1]
    both = dot_nt(query, weights[: 2 * width])
    gate, up = both[:, :width], both[:, width:]
    hidden = (gate * jax.nn.sigmoid(gate) * up).astype(BF16)
    return dot_nn(hidden, weights[2 * width :]).astype(BF16)


def first_kernel(count, *refs):
    blocks, (weight_ref, total_ref) = refs[:count], refs[count:]
    add_gradients(blocks, weight_ref, total_ref)


def second_kernel(block, weight_ref, before_ref, *refs):
    *outs, total_ref = refs
    total_ref[...] = before_ref[...]
    add_gradients((block,), weight_ref, total_ref, first=False)
    write_sums(total_ref, outs)


def update_kernel(*refs):
    updated(refs[:3], refs[3:6], *refs[6:])


def middle_kernel(count, *refs):
    blocks, (weight_ref, *outs, total_ref) = refs[:count], refs[count:]
    add_gradients(blocks, weight_ref, total_ref)
    write_sums(total_ref, outs)


def last_kernel(heads, place_ref, *refs):
    weight_ref, block, query_ref, *outs, next_ref, fast_ref = refs[6:]
    updated(refs[:3], refs[3:6], weight_ref, block, next_ref)
    fast_ref[...] = fast_rows(query_ref[...], next_ref)
    share = fast_ref.shape[0] // heads
    for shift in range(heads):
        to = lax.rem(place_ref[0] + shift, heads)
        outs[shift][...] = fast_ref[pl.ds(pl.multiple_of(to * share, share), share)]


def query_kernel(heads, segments, choices, *refs):
    place_ref, query_ref = refs[:2]
    weight_refs = refs[2 : 1 + segments]
    at = 1 + segments
    owns = refs[at : at + segments]
    at += segments
    cands = [refs[at + s * choices : at + (s + 1) * choices] for s in range(segments)]
    at += segments * choices
    outs = refs[at : at + heads]
    last_query_ref, rows_ref = refs[at + heads :]
    head, place, core = place_ref[0], place_ref[1], place_ref[2]
    width, rows = query_ref.shape[1:]
    share = rows // heads
    scale = 1.0 / math.sqrt(width)
    for s in range(segments):
        query = query_ref[s].T
        if s == segments - 1:
            last_query_ref[...] = query
        else:
            rows_ref[segments + s] = fast_rows(query, weight_refs[s])
        prev = cands[s][choices - 1][: 2 * width]
        if s > 0:
            prev = jnp.where(core == 0, cands[s - 1][choices - 1][: 2 * width], prev)
        for i in range(choices - 1):
            low = lax.rem(place, 2 << i) == (1 << i)
            prev = jnp.where(low, cands[s][i][: 2 * width], prev)
        own = owns[s]
        own_scores = dot_nn(query, own[:width]) * scale
        prev_scores = dot_nn(query, prev[:width]) * scale
        q_at = lax.broadcasted_iota(jnp.int32, (rows, rows), 0)
        k_at = lax.broadcasted_iota(jnp.int32, (rows, rows), 1)
        own_live = (k_at <= q_at) & (k_at > q_at - WINDOW)
        prev_live = k_at - rows > q_at - WINDOW
        if s == 0:
            reach = jnp.where((core == 0) & (place == 0), -rows, 0)
            prev_live = prev_live & (k_at < rows + reach)
        own_scores = jnp.where(own_live, own_scores, -1e30)
        prev_scores = jnp.where(prev_live, prev_scores, -1e30)
        top = jnp.maximum(
            jnp.max(own_scores, axis=-1, keepdims=True),
            jnp.max(prev_scores, axis=-1, keepdims=True),
        )
        own_expo = jnp.exp(own_scores - top)
        prev_expo = jnp.exp(prev_scores - top)
        total = jnp.sum(own_expo, axis=-1, keepdims=True) + jnp.sum(
            prev_expo, axis=-1, keepdims=True
        )
        over = 1.0 / total
        attended = dot_nt((own_expo * over).astype(BF16), own[width : 2 * width]) + dot_nt(
            (prev_expo * over).astype(BF16), prev[width:]
        )
        rows_ref[s] = attended.astype(BF16)
    for shift in range(heads):
        to = lax.rem(head + shift, heads)
        for i in range(2 * segments - 1):
            outs[shift][i] = rows_ref[i, pl.ds(pl.multiple_of(to * share, share), share)]


def normed(parts, gain_row, full_width):
    total = 0.0
    wides = []
    for part in parts:
        wide = part.astype(F32)
        wides.append(wide)
        total = total + jnp.sum(wide * wide, axis=-1, keepdims=True)
    factor = lax.rsqrt(total / full_width + NORM_EPS)
    width = parts[0].shape[1]
    return [
        wide * factor * gain_row[:, i * width : (i + 1) * width] for i, wide in enumerate(wides)
    ]


def early_kernel(heads, segments, me_ref, gain_ref, *refs):
    early, (out_ref, last_ref, held, made, sem) = refs[:heads], refs[heads:]
    width = held.shape[-1]
    me = me_ref[0]
    for k in range(heads):
        held[lax.rem(me - k + heads, heads)] = early[k][...]
    for s in range(segments):
        att = normed([held[j, s] for j in range(heads)], gain_ref[1:2], heads * width)
        if s == segments - 1:
            last_ref[...] = jnp.concatenate(att, -1)
        else:
            fast = [held[j, segments + s] for j in range(heads)]
            fast = normed(fast, gain_ref[0:1], heads * width)
            made[s, 0] = jnp.concatenate([a + b for a, b in zip(fast, att)], -1)
    copy = pltpu.make_async_copy(made, out_ref.at[pl.ds(0, segments - 1)], sem)
    copy.start()
    copy.wait()


def final_kernel(heads, segments, me_ref, gain_ref, out_in_ref, last_ref, *refs):
    late, (out_ref, held, made, sem) = refs[:heads], refs[heads:]
    width = held.shape[-1]
    me = me_ref[0]
    for k in range(heads):
        held[lax.rem(me - k + heads, heads)] = late[k][...]
    fast = normed([held[j] for j in range(heads)], gain_ref[0:1], heads * width)
    made[0, 0] = jnp.concatenate(fast, -1) + last_ref[...]
    copy = pltpu.make_async_copy(made, out_ref.at[pl.ds(segments - 1, 1)], sem)
    copy.start()
    copy.wait()


def on_device(
    query_rows,
    key_rows,
    value_rows,
    token_rates,
    gate_weight,
    up_weight,
    down_weight,
    step_size,
    branch_gains,
    *,
    heads,
    toks,
):
    segments, rows, width = query_rows.shape
    half = toks // 2
    share = rows // heads

    def regroup(h, t):
        return h - h % 2 + t // half, (h % 2) * half + t % half

    def other_core(h, t):
        return h ^ 1, t

    def send(array, where, name):
        with jax.named_scope(name):
            return moved(array, heads, toks, where)

    me = lax.axis_index("head")
    core = me % 2
    tok = lax.axis_index("tok")
    group = tok // half
    place = tok % half
    head_of = me - core + group

    position = jnp.stack([head_of, place, core, (core == group).astype(jnp.int32)])
    position = position.astype(jnp.int32)
    block_shape = jax.ShapeDtypeStruct((2 * width + EXTRA, rows), BF16)
    blocks = call(
        functools.partial(pack_kernel, segments),
        (block_shape,) * segments,
        (turned(key_rows), turned(value_rows), token_rates, step_size),
        (
            pltpu.VMEM((segments, 1, rows), F32),
            pltpu.SMEM((1,), F32),
            pltpu.SemaphoreType.DMA((segments + 1, 2)),
        ),
        loose=(0, 1, 2, 3),
        vmem=56 * 1024 * 1024,
    )
    first = send(blocks[0], regroup, "regroup_0")
    parts = [gate_weight[0], up_weight[0], down_weight[0]]
    lent = [send(part, other_core, f"lend_{i}") for i, part in enumerate(parts)]
    padded = -(-width // 128) * 128
    weight_shape = jax.ShapeDtypeStruct((3 * width, width), BF16)
    weights = call(
        weight_kernel,
        weight_shape,
        (position, *parts, *lent),
        (pltpu.VMEM((3, width, width), BF16), pltpu.SemaphoreType.DMA((3,))),
        smem=(0,),
        loose=range(1, 7),
        vmem=VMEM_BYTES,
    )
    own = [tied(first, weights)]
    for s in range(1, segments):
        own.append(send(tied(blocks[s], own[-1]), regroup, f"regroup_{s}"))
    queries = send(turned(query_rows), regroup, "regroup_queries")

    here = []
    for s in range(segments):
        got = {0: tied(own[s], gate) if s else own[s]}
        step = half // 2
        while step:
            for mask in sorted(got):
                block = got[mask]
                if s == 0 and mask and step == 1:
                    block = gate = tied(block, got[1])
                got[mask | step] = send(
                    block,
                    lambda h, t, step=step: (h, t ^ step),
                    f"gather_{s}_{mask | step}",
                )
            step //= 2
        here.append([got[mask] for mask in range(half)])

    grad_shapes = (jax.ShapeDtypeStruct((width, padded), BF16),) * 3
    total = pltpu.VMEM((3 * width, width), F32)
    grad_flops = 2 * 6 * half * rows * width * width
    ns_flops = 2 * 27 * width**3

    before = call(
        functools.partial(first_kernel, half - 1),
        jax.ShapeDtypeStruct((3 * width, width), F32),
        (*here[0][:-1], weights),
        waits=own[1:],
        flops=grad_flops,
    )
    mine = call(second_kernel, grad_shapes, (here[0][-1], weights, before), (total,))
    all_weights = []
    for s in range(1, segments):
        other = [send(one, other_core, f"swap_{s - 1}") for one in mine]
        weights = call(
            update_kernel,
            weight_shape,
            (*mine, *other, weights, own[s - 1]),
            waits=(queries,),
            flops=ns_flops,
        )
        mine = call(
            functools.partial(middle_kernel, half),
            grad_shapes,
            (*here[s], weights),
            (total,),
            flops=grad_flops,
        )
        all_weights.append(weights)
    other = [send(one, other_core, f"swap_{segments - 1}") for one in mine]

    lasts = [
        send(here[s][half - 1], other_core, f"last_{s}")
        for s in range(segments)
    ]
    cands = []
    for s in range(segments):
        one = []
        mask = 1
        while mask < half:
            one.append(here[s][mask])
            mask = 2 * mask + 1
        cands.append(one + [lasts[s]])
    choices = len(cands[0])
    *early, last_query = call(
        functools.partial(query_kernel, heads, segments, choices),
        tuple(
            jax.ShapeDtypeStruct((2 * segments - 1, share, width), BF16) for _ in range(heads)
        )
        + (jax.ShapeDtypeStruct((rows, width), BF16),),
        (position, queries, *all_weights, *own, *[c for one in cands for c in one]),
        (pltpu.VMEM((2 * segments - 1, rows, width), BF16),),
        smem=(0,),
        flops=2 * segments * 4 * rows * rows * width,
    )
    late = call(
        functools.partial(last_kernel, heads),
        tuple(jax.ShapeDtypeStruct((share, width), BF16) for _ in range(heads)),
        (position, *mine, *other, weights, own[-1], last_query),
        (pltpu.VMEM((3 * width, width), BF16), pltpu.VMEM((rows, width), BF16)),
        smem=(0,),
        flops=ns_flops,
    )

    def spread(parts, name):
        got = []
        for shift in range(heads):

            def where(h, t, shift=shift):
                mine = h - h % 2 + t // half
                return (mine + shift) % heads, (h % 2) * half + t % half

            got.append(send(parts[shift], where, f"{name}_{shift}"))
        return got

    mine_at = me[None].astype(jnp.int32)
    out_shape = jax.ShapeDtypeStruct((segments, 1, share, heads * width), F32)
    begun, last = call(
        functools.partial(early_kernel, heads, segments),
        (out_shape, jax.ShapeDtypeStruct((share, heads * width), F32)),
        (mine_at, branch_gains, *spread(early, "spread_early")),
        (
            pltpu.VMEM((heads, 2 * segments - 1, share, width), BF16),
            pltpu.VMEM((segments - 1, 1, share, heads * width), F32),
            pltpu.SemaphoreType.DMA,
        ),
        smem=(0,),
        loose_out=(0,),
    )
    return call(
        functools.partial(final_kernel, heads, segments),
        out_shape,
        (mine_at, branch_gains, begun, last, *spread(late, "spread_late")),
        (
            pltpu.VMEM((heads, share, width), BF16),
            pltpu.VMEM((1, 1, share, heads * width), F32),
            pltpu.SemaphoreType.DMA,
        ),
        smem=(0,),
        loose=(2,),
        loose_out=(0,),
        aliases={2: 0},
    )


def solution(mesh):
    placed = (
        P(None, "tok", "head"),
        P(None, "tok", "head"),
        P(None, "tok", "head"),
        P(None, "head", "tok"),
        P("head", None, None),
        P("head", None, None),
        P("head", None, None),
        P("head"),
        P(),
    )
    heads, toks = mesh.shape["head"], mesh.shape["tok"]

    def program(*arrays):
        return on_device(*arrays, heads=heads, toks=toks)

    return jax.shard_map(
        program,
        mesh=mesh,
        in_specs=placed,
        out_specs=P(None, "tok", "head", None),
        check_vma=False,
    )
```

```python
import functools
import math

import jax
import jax.numpy as jnp
from jax import lax
from jax.experimental import pallas as pl
from jax.experimental.pallas import tpu as pltpu
from jax.sharding import PartitionSpec as P

WINDOW = 256
NS_STEPS = 3
NEWTON_A = 3.4445
NEWTON_B = -4.775
NEWTON_C = 2.0315
NORM_EPS = 1e-06
FROB_EPS = 1e-07
BOTH = ("head", "tok")
EXTRA = 16
VMEM_BYTES = 20 * 1024 * 1024
F32 = jnp.float32
BF16 = jnp.bfloat16


def moved(array, heads, toks, where):
    pairs = []
    for h in range(heads):
        for t in range(toks):
            to = where(h, t)
            if to is not None:
                pairs.append((h * toks + t, to[0] * toks + to[1]))
    return lax.ppermute(array, BOTH, pairs)


def hold_kernel(in_ref, out_ref):
    out_ref[...] = in_ref[...]


def tied(array, *others):
    shape = jax.ShapeDtypeStruct(array.shape, array.dtype)
    return call(hold_kernel, shape, (array,), waits=others)


def turned(array):
    return jnp.swapaxes(array, 1, 2)


def dot_nn(left, right):
    return jnp.dot(left, right, preferred_element_type=F32)


def dot_nt(left, right):
    return lax.dot_general(left, right, (((1,), (1,)), ((), ())), preferred_element_type=F32)


def call(
    kernel,
    out_shape,
    args,
    scratch=(),
    smem=(),
    loose=(),
    loose_out=(),
    aliases={},
    waits=(),
    vmem=VMEM_BYTES,
    flops=0,
):
    def space(i):
        return pltpu.SMEM if i in smem else pl.ANY if i in loose else pltpu.VMEM

    count = len(args)
    specs = [pl.BlockSpec(memory_space=space(i)) for i in range(count)]
    specs += [pl.BlockSpec(memory_space=pltpu.VMEM) for _ in waits]
    single = not isinstance(out_shape, tuple)
    shapes = (out_shape,) if single else out_shape

    def body(*refs):
        kernel(*refs[:count], *refs[count + len(waits) :])

    outs = pl.pallas_call(
        body,
        out_shape=shapes,
        in_specs=specs,
        out_specs=tuple(
            pl.BlockSpec(memory_space=pl.ANY if i in loose_out else pltpu.VMEM)
            for i in range(len(shapes))
        ),
        scratch_shapes=list(scratch),
        input_output_aliases=aliases,
        compiler_params=pltpu.CompilerParams(vmem_limit_bytes=vmem),
        cost_estimate=pl.CostEstimate(flops=flops, bytes_accessed=1 << 20, transcendentals=0),
    )(*args, *waits)
    return outs[0] if single else outs


def pack_kernel(segments, key_ref, value_ref, rate_ref, step_ref, *refs):
    outs, (held_rate, held_step, sems) = refs[:segments], refs[segments:]
    width, rows = key_ref.shape[1:]
    copies = [
        pltpu.make_async_copy(rate_ref, held_rate, sems.at[segments, 0]),
        pltpu.make_async_copy(step_ref, held_step, sems.at[segments, 1]),
    ]
    for s, out_ref in enumerate(outs):
        for i, ref in enumerate((key_ref, value_ref)):
            copies.append(
                pltpu.make_async_copy(
                    ref.at[s], out_ref.at[pl.ds(i * width, width)], sems.at[s, i]
                )
            )
    for copy in copies:
        copy.start()
    for copy in copies[:2]:
        copy.wait()
    for s, out_ref in enumerate(outs):
        rate = held_rate[s]
        step = jnp.full_like(rate, held_step[0])
        row = lax.broadcasted_iota(jnp.int32, (EXTRA, rows), 0)
        filled = jnp.zeros((EXTRA, rows), F32)
        at = 0
        for value in (rate, step):
            for _ in range(3):
                term = value.astype(BF16).astype(F32)
                filled = jnp.where(row == at, term, filled)
                value = value - term
                at += 1
        out_ref[2 * width :] = filled.astype(BF16)
    for copy in copies[2:]:
        copy.wait()


def weight_kernel(place_ref, *refs):
    mine, other, (out_ref, held, sems) = refs[:3], refs[3:6], refs[6:]
    width = out_ref.shape[1]

    def load(parts):
        copies = [
            pltpu.make_async_copy(ref, held.at[i], sems.at[i]) for i, ref in enumerate(parts)
        ]
        for copy in copies:
            copy.start()
        for copy in copies:
            copy.wait()

    @pl.when(place_ref[3] == 1)
    def _():
        load(mine)

    @pl.when(place_ref[3] != 1)
    def _():
        load(other)

    for i in range(3):
        out_ref[i * width : (i + 1) * width] = held[i].T if i < 2 else held[i]


def add_gradients(blocks, weights, total_ref, first=True):
    width = weights.shape[1]
    for block in blocks:
        keys = block[:width]
        values = block[width : 2 * width]
        terms = block[2 * width :].astype(F32)
        rate = -(terms[0:1] + terms[1:2] + terms[2:3])
        both = dot_nn(weights[: 2 * width], keys)
        gate, up = both[:width], both[width:]
        back = dot_nn(weights[2 * width :], values) * rate
        sig = jax.nn.sigmoid(gate)
        swish = gate * sig
        hidden = (swish * up * rate).astype(BF16)
        d_gate = (back * up * (sig + swish * (1.0 - sig))).astype(BF16)
        d_up = (back * swish).astype(BF16)
        parts = (dot_nt(d_gate, keys), dot_nt(d_up, keys), dot_nt(hidden, values))
        for i, part in enumerate(parts):
            at = pl.ds(i * width, width)
            total_ref[at] = part if first else total_ref[at] + part
        first = False


def symmetric(size, product):
    main = size - size % 256
    if main in (0, size):
        return product(slice(0, size), slice(0, size)).astype(BF16)
    left = product(slice(0, size), slice(0, main))
    corner = product(slice(main, size), slice(main, size)).astype(BF16)
    right = jnp.concatenate([left[main:].T.astype(BF16), corner], 0)
    return jnp.concatenate([left.astype(BF16), right], 1)


def square_of(x):
    return symmetric(x.shape[0], lambda rows, columns: dot_nt(x[rows], x[columns]))


def mixing_of(s):
    def part(rows, columns):
        return NEWTON_B * s[rows, columns].astype(F32) + NEWTON_C * dot_nn(s[rows], s[:, columns])

    return symmetric(s.shape[0], part)


def orthogonalized(totals):
    iterates = []
    for one in totals:
        norm = jnp.sqrt(jnp.sum(one * one, keepdims=True))
        iterates.append((one / (norm + FROB_EPS)).astype(BF16))
    for _ in range(NS_STEPS):
        squares = [square_of(x) for x in iterates]
        mixings = [mixing_of(s) for s in squares]
        iterates = [
            (NEWTON_A * x.astype(F32) + dot_nn(m, x)).astype(BF16)
            for m, x in zip(mixings, iterates)
        ]
    return iterates


def updated(mine, other, weights, step_block, out_ref):
    width = out_ref.shape[1]
    terms = step_block[2 * width :].astype(F32)
    step = (terms[3:4] + terms[4:5] + terms[5:6])[:, 0:1]
    totals = [a[:, :width].astype(F32) + b[:, :width].astype(F32) for a, b in zip(mine, other)]
    for i, x in enumerate(orthogonalized(totals)):
        at = pl.ds(i * width, width)
        out_ref[at] = (weights[at].astype(F32) - step * x.astype(F32)).astype(BF16)


def write_sums(total_ref, outs):
    width = total_ref.shape[1]
    for i, out_ref in enumerate(outs):
        out_ref[:, :width] = total_ref[i * width : (i + 1) * width].astype(BF16)
        out_ref[:, width:] = jnp.zeros((width, out_ref.shape[1] - width), BF16)


def fast_rows(query, weights):
    width = weights.shape[1]
    both = dot_nt(query, weights[: 2 * width])
    gate, up = both[:, :width], both[:, width:]
    hidden = (gate * jax.nn.sigmoid(gate) * up).astype(BF16)
    return dot_nn(hidden, weights[2 * width :]).astype(BF16)


def first_kernel(count, *refs):
    blocks, (weight_ref, total_ref) = refs[:count], refs[count:]
    add_gradients(blocks, weight_ref, total_ref)


def second_kernel(block, weight_ref, before_ref, *refs):
    *outs, total_ref = refs
    total_ref[...] = before_ref[...]
    add_gradients((block,), weight_ref, total_ref, first=False)
    write_sums(total_ref, outs)


def update_kernel(*refs):
    updated(refs[:3], refs[3:6], *refs[6:])


def middle_kernel(count, *refs):
    blocks, (weight_ref, *outs, total_ref) = refs[:count], refs[count:]
    add_gradients(blocks, weight_ref, total_ref)
    write_sums(total_ref, outs)


def last_kernel(heads, place_ref, *refs):
    weight_ref, block, query_ref, *outs, next_ref, fast_ref = refs[6:]
    updated(refs[:3], refs[3:6], weight_ref, block, next_ref)
    fast_ref[...] = fast_rows(query_ref[...], next_ref)
    share = fast_ref.shape[0] // heads
    for shift in range(heads):
        to = lax.rem(place_ref[0] + shift, heads)
        outs[shift][...] = fast_ref[pl.ds(pl.multiple_of(to * share, share), share)]


def query_kernel(heads, segments, choices, *refs):
    place_ref, query_ref = refs[:2]
    weight_refs = refs[2 : 1 + segments]
    at = 1 + segments
    owns = refs[at : at + segments]
    at += segments
    cands = [refs[at + s * choices : at + (s + 1) * choices] for s in range(segments)]
    at += segments * choices
    outs = refs[at : at + heads]
    last_query_ref, rows_ref = refs[at + heads :]
    head, place, core = place_ref[0], place_ref[1], place_ref[2]
    width, rows = query_ref.shape[1:]
    share = rows // heads
    scale = 1.0 / math.sqrt(width)
    for s in range(segments):
        query = query_ref[s].T
        if s == segments - 1:
            last_query_ref[...] = query
        else:
            rows_ref[segments + s] = fast_rows(query, weight_refs[s])
        prev = cands[s][choices - 1][: 2 * width]
        if s > 0:
            prev = jnp.where(core == 0, cands[s - 1][choices - 1][: 2 * width], prev)
        for i in range(choices - 1):
            low = lax.rem(place, 2 << i) == (1 << i)
            prev = jnp.where(low, cands[s][i][: 2 * width], prev)
        own = owns[s]
        own_scores = dot_nn(query, own[:width]) * scale
        prev_scores = dot_nn(query, prev[:width]) * scale
        q_at = lax.broadcasted_iota(jnp.int32, (rows, rows), 0)
        k_at = lax.broadcasted_iota(jnp.int32, (rows, rows), 1)
        own_live = (k_at <= q_at) & (k_at > q_at - WINDOW)
        prev_live = k_at - rows > q_at - WINDOW
        if s == 0:
            reach = jnp.where((core == 0) & (place == 0), -rows, 0)
            prev_live = prev_live & (k_at < rows + reach)
        own_scores = jnp.where(own_live, own_scores, -1e30)
        prev_scores = jnp.where(prev_live, prev_scores, -1e30)
        top = jnp.maximum(
            jnp.max(own_scores, axis=-1, keepdims=True),
            jnp.max(prev_scores, axis=-1, keepdims=True),
        )
        own_expo = jnp.exp(own_scores - top)
        prev_expo = jnp.exp(prev_scores - top)
        total = jnp.sum(own_expo, axis=-1, keepdims=True) + jnp.sum(
            prev_expo, axis=-1, keepdims=True
        )
        over = 1.0 / total
        attended = dot_nt((own_expo * over).astype(BF16), own[width : 2 * width]) + dot_nt(
            (prev_expo * over).astype(BF16), prev[width:]
        )
        rows_ref[s] = attended.astype(BF16)
    for shift in range(heads):
        to = lax.rem(head + shift, heads)
        for i in range(2 * segments - 1):
            outs[shift][i] = rows_ref[i, pl.ds(pl.multiple_of(to * share, share), share)]


def normed(parts, gain_row, full_width):
    total = 0.0
    wides = []
    for part in parts:
        wide = part.astype(F32)
        wides.append(wide)
        total = total + jnp.sum(wide * wide, axis=-1, keepdims=True)
    factor = lax.rsqrt(total / full_width + NORM_EPS)
    width = parts[0].shape[1]
    return [
        wide * factor * gain_row[:, i * width : (i + 1) * width] for i, wide in enumerate(wides)
    ]


def early_kernel(heads, segments, me_ref, gain_ref, *refs):
    early, (out_ref, last_ref, held, made, sem) = refs[:heads], refs[heads:]
    width = held.shape[-1]
    me = me_ref[0]
    for k in range(heads):
        held[lax.rem(me - k + heads, heads)] = early[k][...]
    for s in range(segments):
        att = normed([held[j, s] for j in range(heads)], gain_ref[1:2], heads * width)
        if s == segments - 1:
            last_ref[...] = jnp.concatenate(att, -1)
        else:
            fast = [held[j, segments + s] for j in range(heads)]
            fast = normed(fast, gain_ref[0:1], heads * width)
            made[s, 0] = jnp.concatenate([a + b for a, b in zip(fast, att)], -1)
    copy = pltpu.make_async_copy(made, out_ref.at[pl.ds(0, segments - 1)], sem)
    copy.start()
    copy.wait()


def final_kernel(heads, segments, me_ref, gain_ref, out_in_ref, last_ref, *refs):
    late, (out_ref, held, made, sem) = refs[:heads], refs[heads:]
    width = held.shape[-1]
    me = me_ref[0]
    for k in range(heads):
        held[lax.rem(me - k + heads, heads)] = late[k][...]
    fast = normed([held[j] for j in range(heads)], gain_ref[0:1], heads * width)
    made[0, 0] = jnp.concatenate(fast, -1) + last_ref[...]
    copy = pltpu.make_async_copy(made, out_ref.at[pl.ds(segments - 1, 1)], sem)
    copy.start()
    copy.wait()


def on_device(
    query_rows,
    key_rows,
    value_rows,
    token_rates,
    gate_weight,
    up_weight,
    down_weight,
    step_size,
    branch_gains,
    *,
    heads,
    toks,
):
    segments, rows, width = query_rows.shape
    half = toks // 2
    share = rows // heads

    def regroup(h, t):
        return h - h % 2 + t // half, (h % 2) * half + t % half

    def other_core(h, t):
        return h ^ 1, t

    def send(array, where, name):
        with jax.named_scope(name):
            return moved(array, heads, toks, where)

    me = lax.axis_index("head")
    core = me % 2
    tok = lax.axis_index("tok")
    group = tok // half
    place = tok % half
    head_of = me - core + group

    position = jnp.stack([head_of, place, core, (core == group).astype(jnp.int32)])
    position = position.astype(jnp.int32)
    block_shape = jax.ShapeDtypeStruct((2 * width + EXTRA, rows), BF16)
    blocks = call(
        functools.partial(pack_kernel, segments),
        (block_shape,) * segments,
        (turned(key_rows), turned(value_rows), token_rates, step_size),
        (
            pltpu.VMEM((segments, 1, rows), F32),
            pltpu.SMEM((1,), F32),
            pltpu.SemaphoreType.DMA((segments + 1, 2)),
        ),
        loose=(0, 1, 2, 3),
        vmem=56 * 1024 * 1024,
    )
    first = send(blocks[0], regroup, "regroup_0")
    parts = [gate_weight[0], up_weight[0], down_weight[0]]
    lent = [send(part, other_core, f"lend_{i}") for i, part in enumerate(parts)]
    padded = -(-width // 128) * 128
    weight_shape = jax.ShapeDtypeStruct((3 * width, width), BF16)
    weights = call(
        weight_kernel,
        weight_shape,
        (position, *parts, *lent),
        (pltpu.VMEM((3, width, width), BF16), pltpu.SemaphoreType.DMA((3,))),
        smem=(0,),
        loose=range(1, 7),
        vmem=VMEM_BYTES,
    )
    own = [tied(first, weights)]
    for s in range(1, segments):
        own.append(send(tied(blocks[s], own[-1]), regroup, f"regroup_{s}"))
    queries = send(turned(query_rows), regroup, "regroup_queries")

    here = []
    for s in range(segments):
        got = {0: tied(own[s], gate) if s else own[s]}
        step = half // 2
        while step:
            for mask in sorted(got):
                block = got[mask]
                if s == 0 and mask and step == 1:
                    block = gate = tied(block, got[1])
                got[mask | step] = send(
                    block,
                    lambda h, t, step=step: (h, t ^ step),
                    f"gather_{s}_{mask | step}",
                )
            step //= 2
        here.append([got[mask] for mask in range(half)])

    grad_shapes = (jax.ShapeDtypeStruct((width, padded), BF16),) * 3
    total = pltpu.VMEM((3 * width, width), F32)
    grad_flops = 2 * 6 * half * rows * width * width
    ns_flops = 2 * 27 * width**3

    before = call(
        functools.partial(first_kernel, half - 1),
        jax.ShapeDtypeStruct((3 * width, width), F32),
        (*here[0][:-1], weights),
        waits=own[1:],
        flops=grad_flops,
    )
    mine = call(second_kernel, grad_shapes, (here[0][-1], weights, before), (total,))
    all_weights = []
    for s in range(1, segments):
        other = [send(one, other_core, f"swap_{s - 1}") for one in mine]
        weights = call(
            update_kernel,
            weight_shape,
            (*mine, *other, weights, own[s - 1]),
            waits=(queries,),
            flops=ns_flops,
        )
        mine = call(
            functools.partial(middle_kernel, half),
            grad_shapes,
            (*here[s], weights),
            (total,),
            flops=grad_flops,
        )
        all_weights.append(weights)
    other = [send(one, other_core, f"swap_{segments - 1}") for one in mine]

    lasts = [
        send(here[s][half - 1], other_core, f"last_{s}")
        for s in range(segments)
    ]
    cands = []
    for s in range(segments):
        one = []
        mask = 1
        while mask < half:
            one.append(here[s][mask])
            mask = 2 * mask + 1
        cands.append(one + [lasts[s]])
    choices = len(cands[0])
    *early, last_query = call(
        functools.partial(query_kernel, heads, segments, choices),
        tuple(
            jax.ShapeDtypeStruct((2 * segments - 1, share, width), BF16) for _ in range(heads)
        )
        + (jax.ShapeDtypeStruct((rows, width), BF16),),
        (position, queries, *all_weights, *own, *[c for one in cands for c in one]),
        (pltpu.VMEM((2 * segments - 1, rows, width), BF16),),
        smem=(0,),
        flops=2 * segments * 4 * rows * rows * width,
    )
    late = call(
        functools.partial(last_kernel, heads),
        tuple(jax.ShapeDtypeStruct((share, width), BF16) for _ in range(heads)),
        (position, *mine, *other, weights, own[-1], last_query),
        (pltpu.VMEM((3 * width, width), BF16), pltpu.VMEM((rows, width), BF16)),
        smem=(0,),
        flops=ns_flops,
    )

    def spread(parts, name):
        got = []
        for shift in range(heads):

            def where(h, t, shift=shift):
                mine = h - h % 2 + t // half
                return (mine + shift) % heads, (h % 2) * half + t % half

            got.append(send(parts[shift], where, f"{name}_{shift}"))
        return got

    mine_at = me[None].astype(jnp.int32)
    out_shape = jax.ShapeDtypeStruct((segments, 1, share, heads * width), F32)
    begun, last = call(
        functools.partial(early_kernel, heads, segments),
        (out_shape, jax.ShapeDtypeStruct((share, heads * width), F32)),
        (mine_at, branch_gains, *spread(early, "spread_early")),
        (
            pltpu.VMEM((heads, 2 * segments - 1, share, width), BF16),
            pltpu.VMEM((segments - 1, 1, share, heads * width), F32),
            pltpu.SemaphoreType.DMA,
        ),
        smem=(0,),
        loose_out=(0,),
    )
    return call(
        functools.partial(final_kernel, heads, segments),
        out_shape,
        (mine_at, branch_gains, begun, last, *spread(late, "spread_late")),
        (
            pltpu.VMEM((heads, share, width), BF16),
            pltpu.VMEM((1, 1, share, heads * width), F32),
            pltpu.SemaphoreType.DMA,
        ),
        smem=(0,),
        loose=(2,),
        loose_out=(0,),
        aliases={2: 0},
    )


def solution(mesh):
    placed = (
        P(None, "tok", "head"),
        P(None, "tok", "head"),
        P(None, "tok", "head"),
        P(None, "head", "tok"),
        P("head", None, None),
        P("head", None, None),
        P("head", None, None),
        P("head"),
        P(),
    )
    heads, toks = mesh.shape["head"], mesh.shape["tok"]

    def program(*arrays):
        return on_device(*arrays, heads=heads, toks=toks)

    return jax.shard_map(
        program,
        mesh=mesh,
        in_specs=placed,
        out_specs=P(None, "tok", "head", None),
        check_vma=False,
    )
```

```python
import functools
import math

import jax
import jax.numpy as jnp
from jax import lax
from jax.experimental import pallas as pl
from jax.experimental.pallas import tpu as pltpu
from jax.sharding import PartitionSpec as P

WINDOW = 256
NS_STEPS = 3
NEWTON_A = 3.4445
NEWTON_B = -4.775
NEWTON_C = 2.0315
NORM_EPS = 1e-06
FROB_EPS = 1e-07
BOTH = ("head", "tok")
EXTRA = 16
VMEM_BYTES = 20 * 1024 * 1024
F32 = jnp.float32
BF16 = jnp.bfloat16


def moved(array, heads, toks, where):
    pairs = []
    for h in range(heads):
        for t in range(toks):
            to = where(h, t)
            if to is not None:
                pairs.append((h * toks + t, to[0] * toks + to[1]))
    return lax.ppermute(array, BOTH, pairs)


def hold_kernel(in_ref, out_ref):
    out_ref[...] = in_ref[...]


def tied(array, *others):
    shape = jax.ShapeDtypeStruct(array.shape, array.dtype)
    return call(hold_kernel, shape, (array,), waits=others)


def turned(array):
    return jnp.swapaxes(array, 1, 2)


def dot_nn(left, right):
    return jnp.dot(left, right, preferred_element_type=F32)


def dot_nt(left, right):
    return lax.dot_general(left, right, (((1,), (1,)), ((), ())), preferred_element_type=F32)


def call(
    kernel,
    out_shape,
    args,
    scratch=(),
    smem=(),
    loose=(),
    loose_out=(),
    aliases={},
    waits=(),
    vmem=VMEM_BYTES,
    flops=0,
):
    def space(i):
        return pltpu.SMEM if i in smem else pl.ANY if i in loose else pltpu.VMEM

    count = len(args)
    specs = [pl.BlockSpec(memory_space=space(i)) for i in range(count)]
    specs += [pl.BlockSpec(memory_space=pltpu.VMEM) for _ in waits]
    single = not isinstance(out_shape, tuple)
    shapes = (out_shape,) if single else out_shape

    def body(*refs):
        kernel(*refs[:count], *refs[count + len(waits) :])

    outs = pl.pallas_call(
        body,
        out_shape=shapes,
        in_specs=specs,
        out_specs=tuple(
            pl.BlockSpec(memory_space=pl.ANY if i in loose_out else pltpu.VMEM)
            for i in range(len(shapes))
        ),
        scratch_shapes=list(scratch),
        input_output_aliases=aliases,
        compiler_params=pltpu.CompilerParams(vmem_limit_bytes=vmem),
        cost_estimate=pl.CostEstimate(flops=flops, bytes_accessed=1 << 20, transcendentals=0),
    )(*args, *waits)
    return outs[0] if single else outs


def pack_kernel(segments, key_ref, value_ref, rate_ref, step_ref, *refs):
    outs, (held_rate, held_step, sems) = refs[:segments], refs[segments:]
    width, rows = key_ref.shape[1:]
    copies = [
        pltpu.make_async_copy(rate_ref, held_rate, sems.at[segments, 0]),
        pltpu.make_async_copy(step_ref, held_step, sems.at[segments, 1]),
    ]
    for s, out_ref in enumerate(outs):
        for i, ref in enumerate((key_ref, value_ref)):
            copies.append(
                pltpu.make_async_copy(
                    ref.at[s], out_ref.at[pl.ds(i * width, width)], sems.at[s, i]
                )
            )
    for copy in copies:
        copy.start()
    for copy in copies[:2]:
        copy.wait()
    for s, out_ref in enumerate(outs):
        rate = held_rate[s]
        step = jnp.full_like(rate, held_step[0])
        row = lax.broadcasted_iota(jnp.int32, (EXTRA, rows), 0)
        filled = jnp.zeros((EXTRA, rows), F32)
        at = 0
        for value in (rate, step):
            for _ in range(3):
                term = value.astype(BF16).astype(F32)
                filled = jnp.where(row == at, term, filled)
                value = value - term
                at += 1
        out_ref[2 * width :] = filled.astype(BF16)
    for copy in copies[2:]:
        copy.wait()


def weight_kernel(place_ref, *refs):
    mine, other, (out_ref, held, sems) = refs[:3], refs[3:6], refs[6:]
    width = out_ref.shape[1]

    def load(parts):
        copies = [
            pltpu.make_async_copy(ref, held.at[i], sems.at[i]) for i, ref in enumerate(parts)
        ]
        for copy in copies:
            copy.start()
        for copy in copies:
            copy.wait()

    @pl.when(place_ref[3] == 1)
    def _():
        load(mine)

    @pl.when(place_ref[3] != 1)
    def _():
        load(other)

    for i in range(3):
        out_ref[i * width : (i + 1) * width] = held[i].T if i < 2 else held[i]


def add_gradients(blocks, weights, total_ref, first=True):
    width = weights.shape[1]
    for block in blocks:
        keys = block[:width]
        values = block[width : 2 * width]
        terms = block[2 * width :].astype(F32)
        rate = -(terms[0:1] + terms[1:2] + terms[2:3])
        both = dot_nn(weights[: 2 * width], keys)
        gate, up = both[:width], both[width:]
        back = dot_nn(weights[2 * width :], values) * rate
        sig = jax.nn.sigmoid(gate)
        swish = gate * sig
        hidden = (swish * up * rate).astype(BF16)
        d_gate = (back * up * (sig + swish * (1.0 - sig))).astype(BF16)
        d_up = (back * swish).astype(BF16)
        parts = (dot_nt(d_gate, keys), dot_nt(d_up, keys), dot_nt(hidden, values))
        for i, part in enumerate(parts):
            at = pl.ds(i * width, width)
            total_ref[at] = part if first else total_ref[at] + part
        first = False


def symmetric(size, product):
    main = size - size % 256
    if main in (0, size):
        return product(slice(0, size), slice(0, size)).astype(BF16)
    left = product(slice(0, size), slice(0, main)).astype(BF16)
    corner = product(slice(main, size), slice(main, size)).astype(BF16)
    right = jnp.concatenate([left[main:].T, corner], 0)
    return jnp.concatenate([left, right], 1)


def square_of(x):
    return symmetric(x.shape[0], lambda rows, columns: dot_nt(x[rows], x[columns]))


def mixing_of(s):
    def part(rows, columns):
        return NEWTON_B * s[rows, columns].astype(F32) + NEWTON_C * dot_nn(s[rows], s[:, columns])

    return symmetric(s.shape[0], part)


def orthogonalized(totals):
    iterates = []
    for one in totals:
        norm = jnp.sqrt(jnp.sum(one * one, keepdims=True))
        iterates.append((one / (norm + FROB_EPS)).astype(BF16))
    for _ in range(NS_STEPS):
        squares = [square_of(x) for x in iterates]
        mixings = [mixing_of(s) for s in squares]
        iterates = [
            (NEWTON_A * x.astype(F32) + dot_nn(m, x)).astype(BF16)
            for m, x in zip(mixings, iterates)
        ]
    return iterates


def updated(mine, other, weights, step_block, out_ref):
    width = out_ref.shape[1]
    terms = step_block[2 * width :].astype(F32)
    step = (terms[3:4] + terms[4:5] + terms[5:6])[:, 0:1]
    totals = [a[:, :width].astype(F32) + b[:, :width].astype(F32) for a, b in zip(mine, other)]
    for i, x in enumerate(orthogonalized(totals)):
        at = pl.ds(i * width, width)
        out_ref[at] = (weights[at].astype(F32) - step * x.astype(F32)).astype(BF16)


def write_sums(total_ref, outs):
    width = total_ref.shape[1]
    for i, out_ref in enumerate(outs):
        out_ref[:, :width] = total_ref[i * width : (i + 1) * width].astype(BF16)
        out_ref[:, width:] = jnp.zeros((width, out_ref.shape[1] - width), BF16)


def fast_rows(query, weights):
    width = weights.shape[1]
    both = dot_nt(query, weights[: 2 * width])
    gate, up = both[:, :width], both[:, width:]
    hidden = (gate * jax.nn.sigmoid(gate) * up).astype(BF16)
    return dot_nn(hidden, weights[2 * width :]).astype(BF16)


def first_kernel(count, *refs):
    blocks, (weight_ref, total_ref) = refs[:count], refs[count:]
    add_gradients(blocks, weight_ref, total_ref)


def second_kernel(block, weight_ref, before_ref, *refs):
    *outs, total_ref = refs
    total_ref[...] = before_ref[...]
    add_gradients((block,), weight_ref, total_ref, first=False)
    write_sums(total_ref, outs)


def update_kernel(*refs):
    updated(refs[:3], refs[3:6], *refs[6:])


def middle_kernel(count, *refs):
    blocks, (weight_ref, *outs, total_ref) = refs[:count], refs[count:]
    add_gradients(blocks, weight_ref, total_ref)
    write_sums(total_ref, outs)


def last_kernel(heads, place_ref, *refs):
    weight_ref, block, query_ref, *outs, next_ref, fast_ref = refs[6:]
    updated(refs[:3], refs[3:6], weight_ref, block, next_ref)
    fast_ref[...] = fast_rows(query_ref[...], next_ref)
    share = fast_ref.shape[0] // heads
    for shift in range(heads):
        to = lax.rem(place_ref[0] + shift, heads)
        outs[shift][...] = fast_ref[pl.ds(pl.multiple_of(to * share, share), share)]


def query_kernel(heads, segments, choices, *refs):
    place_ref, query_ref = refs[:2]
    weight_refs = refs[2 : 1 + segments]
    at = 1 + segments
    owns = refs[at : at + segments]
    at += segments
    cands = [refs[at + s * choices : at + (s + 1) * choices] for s in range(segments)]
    at += segments * choices
    outs = refs[at : at + heads]
    last_query_ref, rows_ref = refs[at + heads :]
    head, place, core = place_ref[0], place_ref[1], place_ref[2]
    width, rows = query_ref.shape[1:]
    share = rows // heads
    scale = 1.0 / math.sqrt(width)
    for s in range(segments):
        query = query_ref[s].T
        if s == segments - 1:
            last_query_ref[...] = query
        else:
            rows_ref[segments + s] = fast_rows(query, weight_refs[s])
        prev = cands[s][choices - 1][: 2 * width]
        if s > 0:
            prev = jnp.where(core == 0, cands[s - 1][choices - 1][: 2 * width], prev)
        for i in range(choices - 1):
            low = lax.rem(place, 2 << i) == (1 << i)
            prev = jnp.where(low, cands[s][i][: 2 * width], prev)
        own = owns[s]
        own_scores = dot_nn(query, own[:width]) * scale
        prev_scores = dot_nn(query, prev[:width]) * scale
        q_at = lax.broadcasted_iota(jnp.int32, (rows, rows), 0)
        k_at = lax.broadcasted_iota(jnp.int32, (rows, rows), 1)
        own_live = (k_at <= q_at) & (k_at > q_at - WINDOW)
        prev_live = k_at - rows > q_at - WINDOW
        if s == 0:
            reach = jnp.where((core == 0) & (place == 0), -rows, 0)
            prev_live = prev_live & (k_at < rows + reach)
        own_scores = jnp.where(own_live, own_scores, -1e30)
        prev_scores = jnp.where(prev_live, prev_scores, -1e30)
        top = jnp.maximum(
            jnp.max(own_scores, axis=-1, keepdims=True),
            jnp.max(prev_scores, axis=-1, keepdims=True),
        )
        own_expo = jnp.exp(own_scores - top)
        prev_expo = jnp.exp(prev_scores - top)
        total = jnp.sum(own_expo, axis=-1, keepdims=True) + jnp.sum(
            prev_expo, axis=-1, keepdims=True
        )
        over = 1.0 / total
        attended = dot_nt((own_expo * over).astype(BF16), own[width : 2 * width]) + dot_nt(
            (prev_expo * over).astype(BF16), prev[width:]
        )
        rows_ref[s] = attended.astype(BF16)
    for shift in range(heads):
        to = lax.rem(head + shift, heads)
        for i in range(2 * segments - 1):
            outs[shift][i] = rows_ref[i, pl.ds(pl.multiple_of(to * share, share), share)]


def normed(parts, gain_row, full_width):
    total = 0.0
    wides = []
    for part in parts:
        wide = part.astype(F32)
        wides.append(wide)
        total = total + jnp.sum(wide * wide, axis=-1, keepdims=True)
    factor = lax.rsqrt(total / full_width + NORM_EPS)
    width = parts[0].shape[1]
    return [
        wide * factor * gain_row[:, i * width : (i + 1) * width] for i, wide in enumerate(wides)
    ]


def early_kernel(heads, segments, me_ref, gain_ref, *refs):
    early, (out_ref, last_ref, held, made, sem) = refs[:heads], refs[heads:]
    width = held.shape[-1]
    me = me_ref[0]
    for k in range(heads):
        held[lax.rem(me - k + heads, heads)] = early[k][...]
    for s in range(segments):
        att = normed([held[j, s] for j in range(heads)], gain_ref[1:2], heads * width)
        if s == segments - 1:
            last_ref[...] = jnp.concatenate(att, -1)
        else:
            fast = [held[j, segments + s] for j in range(heads)]
            fast = normed(fast, gain_ref[0:1], heads * width)
            made[s, 0] = jnp.concatenate([a + b for a, b in zip(fast, att)], -1)
    copy = pltpu.make_async_copy(made, out_ref.at[pl.ds(0, segments - 1)], sem)
    copy.start()
    copy.wait()


def final_kernel(heads, segments, me_ref, gain_ref, out_in_ref, last_ref, *refs):
    late, (out_ref, held, made, sem) = refs[:heads], refs[heads:]
    width = held.shape[-1]
    me = me_ref[0]
    for k in range(heads):
        held[lax.rem(me - k + heads, heads)] = late[k][...]
    fast = normed([held[j] for j in range(heads)], gain_ref[0:1], heads * width)
    made[0, 0] = jnp.concatenate(fast, -1) + last_ref[...]
    copy = pltpu.make_async_copy(made, out_ref.at[pl.ds(segments - 1, 1)], sem)
    copy.start()
    copy.wait()


def on_device(
    query_rows,
    key_rows,
    value_rows,
    token_rates,
    gate_weight,
    up_weight,
    down_weight,
    step_size,
    branch_gains,
    *,
    heads,
    toks,
):
    segments, rows, width = query_rows.shape
    half = toks // 2
    share = rows // heads

    def regroup(h, t):
        return h - h % 2 + t // half, (h % 2) * half + t % half

    def other_core(h, t):
        return h ^ 1, t

    def send(array, where, name):
        with jax.named_scope(name):
            return moved(array, heads, toks, where)

    me = lax.axis_index("head")
    core = me % 2
    tok = lax.axis_index("tok")
    group = tok // half
    place = tok % half
    head_of = me - core + group

    position = jnp.stack([head_of, place, core, (core == group).astype(jnp.int32)])
    position = position.astype(jnp.int32)
    block_shape = jax.ShapeDtypeStruct((2 * width + EXTRA, rows), BF16)
    blocks = call(
        functools.partial(pack_kernel, segments),
        (block_shape,) * segments,
        (turned(key_rows), turned(value_rows), token_rates, step_size),
        (
            pltpu.VMEM((segments, 1, rows), F32),
            pltpu.SMEM((1,), F32),
            pltpu.SemaphoreType.DMA((segments + 1, 2)),
        ),
        loose=(0, 1, 2, 3),
        vmem=56 * 1024 * 1024,
    )
    first = send(blocks[0], regroup, "regroup_0")
    parts = [gate_weight[0], up_weight[0], down_weight[0]]
    lent = [send(part, other_core, f"lend_{i}") for i, part in enumerate(parts)]
    padded = -(-width // 128) * 128
    weight_shape = jax.ShapeDtypeStruct((3 * width, width), BF16)
    weights = call(
        weight_kernel,
        weight_shape,
        (position, *parts, *lent),
        (pltpu.VMEM((3, width, width), BF16), pltpu.SemaphoreType.DMA((3,))),
        smem=(0,),
        loose=range(1, 7),
        vmem=VMEM_BYTES,
    )
    own = [tied(first, weights)]
    for s in range(1, segments):
        own.append(send(tied(blocks[s], own[-1]), regroup, f"regroup_{s}"))
    queries = send(turned(query_rows), regroup, "regroup_queries")

    def gathered(s, block, others):
        got = {0: block}
        step = half // 2
        while step:
            for mask in sorted(got):
                one = got[mask]
                if mask and step == 1:
                    one = gates[s] = tied(one, *(others or [got[1]]))
                got[mask | step] = send(
                    one, lambda h, t, step=step: (h, t ^ step), f"gather_{s}_{mask | step}"
                )
            step //= 2
        return [got[mask] for mask in range(half)]

    gates = {}
    here = [gathered(0, own[0], [])]
    grad_shapes = (jax.ShapeDtypeStruct((width, padded), BF16),) * 3
    total = pltpu.VMEM((3 * width, width), F32)
    grad_flops = 2 * 6 * half * rows * width * width
    ns_flops = 2 * 27 * width**3

    before = call(
        functools.partial(first_kernel, half - 1),
        jax.ShapeDtypeStruct((3 * width, width), F32),
        (*here[0][:-1], weights),
        waits=own[1:],
        flops=grad_flops,
    )
    for s in range(1, segments):
        here.append(gathered(s, tied(own[s], gates[0]), [before]))
    mine = call(second_kernel, grad_shapes, (here[0][-1], weights, before), (total,))
    all_weights = []
    for s in range(1, segments):
        other = [send(one, other_core, f"swap_{s - 1}") for one in mine]
        weights = call(
            update_kernel,
            weight_shape,
            (*mine, *other, weights, own[s - 1]),
            waits=(queries,),
            flops=ns_flops,
        )
        mine = call(
            functools.partial(middle_kernel, half),
            grad_shapes,
            (*here[s], weights),
            (total,),
            flops=grad_flops,
        )
        all_weights.append(weights)
    other = [send(one, other_core, f"swap_{segments - 1}") for one in mine]

    lasts = [
        send(here[s][half - 1], other_core, f"last_{s}")
        for s in range(segments)
    ]
    cands = []
    for s in range(segments):
        one = []
        mask = 1
        while mask < half:
            one.append(here[s][mask])
            mask = 2 * mask + 1
        cands.append(one + [lasts[s]])
    choices = len(cands[0])
    *early, last_query = call(
        functools.partial(query_kernel, heads, segments, choices),
        tuple(
            jax.ShapeDtypeStruct((2 * segments - 1, share, width), BF16) for _ in range(heads)
        )
        + (jax.ShapeDtypeStruct((rows, width), BF16),),
        (position, queries, *all_weights, *own, *[c for one in cands for c in one]),
        (pltpu.VMEM((2 * segments - 1, rows, width), BF16),),
        smem=(0,),
        flops=2 * segments * 4 * rows * rows * width,
    )
    late = call(
        functools.partial(last_kernel, heads),
        tuple(jax.ShapeDtypeStruct((share, width), BF16) for _ in range(heads)),
        (position, *mine, *other, weights, own[-1], last_query),
        (pltpu.VMEM((3 * width, width), BF16), pltpu.VMEM((rows, width), BF16)),
        smem=(0,),
        flops=ns_flops,
    )

    def spread(parts, name):
        got = []
        for shift in range(heads):

            def where(h, t, shift=shift):
                mine = h - h % 2 + t // half
                return (mine + shift) % heads, (h % 2) * half + t % half

            got.append(send(parts[shift], where, f"{name}_{shift}"))
        return got

    mine_at = me[None].astype(jnp.int32)
    out_shape = jax.ShapeDtypeStruct((segments, 1, share, heads * width), F32)
    begun, last = call(
        functools.partial(early_kernel, heads, segments),
        (out_shape, jax.ShapeDtypeStruct((share, heads * width), F32)),
        (mine_at, branch_gains, *spread(early, "spread_early")),
        (
            pltpu.VMEM((heads, 2 * segments - 1, share, width), BF16),
            pltpu.VMEM((segments - 1, 1, share, heads * width), F32),
            pltpu.SemaphoreType.DMA,
        ),
        smem=(0,),
        loose_out=(0,),
    )
    return call(
        functools.partial(final_kernel, heads, segments),
        out_shape,
        (mine_at, branch_gains, begun, last, *spread(late, "spread_late")),
        (
            pltpu.VMEM((heads, share, width), BF16),
            pltpu.VMEM((1, 1, share, heads * width), F32),
            pltpu.SemaphoreType.DMA,
        ),
        smem=(0,),
        loose=(2,),
        loose_out=(0,),
        aliases={2: 0},
    )


def solution(mesh):
    placed = (
        P(None, "tok", "head"),
        P(None, "tok", "head"),
        P(None, "tok", "head"),
        P(None, "head", "tok"),
        P("head", None, None),
        P("head", None, None),
        P("head", None, None),
        P("head"),
        P(),
    )
    heads, toks = mesh.shape["head"], mesh.shape["tok"]

    def program(*arrays):
        return on_device(*arrays, heads=heads, toks=toks)

    return jax.shard_map(
        program,
        mesh=mesh,
        in_specs=placed,
        out_specs=P(None, "tok", "head", None),
        check_vma=False,
    )
```
